256 devices in a mesh: row: 16 (over x_lo, z), rep: 8 (over x_hi, y), feat: 2 (over core).
Axes of the slice: x: 4 (x_hi: 2, x_lo: 2; x = x_hi * 2 + x_lo), y: 4, z: 8, core: 2. Of those that a mesh axis runs over, the one named last changes fastest.
Arguments:
- features: bfloat16 [32768, 512], P('row', 'feat'), may hold values from -6 to 6
- grad_out: bfloat16 [32768, 512], P('row', 'feat'), may hold values from -6 to 6
- relu_mask: int32 [32768, 512], P('row', 'feat'), may hold values 0 or 1
- block_columns: int32 [256, 128], P('row', 'rep'), may hold values from 0 to 255, as said below
- block_count: int32 [256], P('row'), may hold values from 1 to 128, as said below
- block_weights: bfloat16 [256, 128, 128, 128], P('row', 'rep'), may hold values from -0.0625 to 0.0625
- self_weight: bfloat16 [512, 512], P('feat'), may hold values from -0.25 to 0.25
- neighbor_weight: bfloat16 [512, 512], P('feat'), may hold values from -0.25 to 0.25
Outputs:
- features_grad: float32 [32768, 512], P(('row', 'rep'), 'feat')
- self_grad: float32 [512, 512], P('feat')
- neighbor_grad: float32 [512, 512], P('feat')
The draws below stay inside these ranges and needn't reach their ends.
Inputs may be any that keep to these rules, and one draw needn't show every extreme that they name: block_columns[b, k] is a block of the index of row that holds block row b, or of the index just before or just after it, the last index of row and the first being neighbours; each index of row holds 16 consecutive blocks. Block row b uses slots 0 to block_count[b] - 1; the other slots are ignored.
All inputs are finite; a program needn't handle non-finite values. No bound on the sum of `relu_mask` on one device may be relied on, other than what follows from the above.
Results may differ from the reference program's by a relative error of at most 0.0034.
Values may be sent and summed in bfloat16 or wider, within the bound.
No kernel may reach another device: no remote copies, remote signals or barrier semaphores. Data moves between devices by JAX's collectives and lax.ppermute only.
A program may use at most 192 MiB of HBM per device.

```python
import jax
import jax.numpy as jnp
from jax import lax

D_IN = 512
D_OUT = 512
BLOCK = 128
BLK_DEV = 16
NBLK = 256
KB = 128
NODES = 32768


def draw_block_columns(key, part):
    key = jax.random.fold_in(key, 11)
    key_offset, key_local = jax.random.split(key)
    devices_count = NBLK // BLK_DEV
    owners = jnp.arange(NBLK, dtype=jnp.int32) // BLK_DEV
    offsets = jax.random.randint(key_offset, (NBLK, KB), -1, 2, dtype=jnp.int32)
    local_blocks = jax.random.randint(key_local, (NBLK, KB), 0, BLK_DEV, dtype=jnp.int32)
    chosen = (owners[:, None] + offsets) % devices_count * BLK_DEV + local_blocks
    chosen = chosen.at[0, 0].set(NBLK - 1).at[0, 1].set(0)
    return chosen.astype(jnp.int32)


def draw_block_count(key, part):
    key = jax.random.fold_in(key, 13)
    counts = jax.random.randint(key, (NBLK,), 1, KB + 1, dtype=jnp.int32)
    counts = counts.at[0].set(KB).at[1].set(1)
    return counts.astype(jnp.int32)


def with_ends(drawn, key, low, top_value):
    extent = drawn.shape
    place = [jax.random.randint(jax.random.fold_in(key, axis), (), 0, extent[axis]) for axis in range(len(extent))]
    drawn = drawn.at[tuple(place)].set(low)
    longest = extent.index(max(extent))
    place[longest] = (place[longest] + 1) % extent[longest]
    return drawn.at[tuple(place)].set(top_value)


def level_of(rng, shape, cuts, smallest, high):
    def one(axis_at, blocks):
        heights = jax.random.uniform(jax.random.fold_in(jax.random.fold_in(rng, 6), axis_at), (blocks,), jnp.float32, smallest / len(cuts), high / len(cuts))
        return jnp.repeat(jnp.exp(heights), shape[axis_at] // blocks).reshape((-1,) + (1,) * (len(shape) - axis_at - 1))

    loudness = one(*cuts[0])
    for cut in cuts[1:]:
        loudness = loudness * one(*cut)
    return loudness


def bell_draw(rng, extent, spread, bound, pieces=(), held_as=jnp.bfloat16):
    entries = jax.random.normal(rng, extent, jnp.float32) * spread
    if len(pieces) > 0:
        entries = level_of(rng, extent, pieces, -0.22, 0.18) * entries
    return jnp.clip(entries, min=-bound, max=bound).astype(held_as)


def setup_inputs(seed: int = 0) -> dict:
    key_list = jax.random.split(jax.random.key(seed), 9)
    features = bell_draw(key_list[0], (NODES, D_IN), 1.0, 6.0, ((0, 16), (1, 2)))
    grad_out = bell_draw(key_list[1], (NODES, D_OUT), 1.0, 6.0, ((0, 16), (1, 2)))
    relu_mask = with_ends((jax.random.randint(key_list[2], (NODES, D_OUT), 0, 2) < 1).astype(jnp.int32), jax.random.fold_in(key_list[2], 1), 0, 1)
    block_columns = draw_block_columns(jax.random.fold_in(key_list[8], 71), 0)
    block_count = draw_block_count(jax.random.fold_in(key_list[8], 71), 0)
    block_weights = bell_draw(key_list[5], (NBLK, KB, BLOCK, BLOCK), (64 * KB) ** -0.5, 0.0625, ((0, 16), (1, 8)))
    self_weight = bell_draw(key_list[6], (D_IN, D_OUT), D_OUT ** -0.5, 0.25, ((0, 2),))
    neighbor_weight = bell_draw(key_list[7], (D_IN, D_OUT), D_OUT ** -0.5, 0.25, ((0, 2),))
    return {"features": features, "grad_out": grad_out, "relu_mask": relu_mask, "block_columns": block_columns, "block_count": block_count, "block_weights": block_weights, "self_weight": self_weight, "neighbor_weight": neighbor_weight}


def reference(features, grad_out, relu_mask, block_columns, block_count, block_weights, self_weight, neighbor_weight):
    block_rows, slot_width = block_columns.shape
    feature_width = features.shape[1]
    slot_range = jnp.arange(slot_width, dtype=jnp.int32)
    feature_blocks = features.reshape(block_rows, BLOCK, feature_width)

    def row_weights(index):
        keep_slot = slot_range < block_count[index]
        weights_row = block_weights[index]
        return jnp.where(keep_slot[:, None, None], weights_row, jnp.zeros_like(weights_row)).astype(jnp.float32)

    def aggregate_row(index):
        sources = feature_blocks[block_columns[index]].astype(jnp.float32)
        return jnp.einsum("kij,kjd->id", row_weights(index), sources).astype(jnp.bfloat16)

    aggregate = lax.map(aggregate_row, jnp.arange(block_rows, dtype=jnp.int32)).reshape(NODES, feature_width)
    masked_grad = grad_out * relu_mask.astype(jnp.bfloat16)
    self_term = jnp.dot(masked_grad, self_weight.T, preferred_element_type=jnp.float32)
    neighbor_term = jnp.dot(masked_grad, neighbor_weight.T, preferred_element_type=jnp.float32).astype(jnp.bfloat16)
    term_blocks = neighbor_term.reshape(block_rows, BLOCK, feature_width)

    def scatter_row(index, scattered):
        contributions = jnp.einsum("kij,id->kjd", row_weights(index), term_blocks[index].astype(jnp.float32))
        return scattered.at[block_columns[index]].add(contributions)

    scattered = lax.fori_loop(0, block_rows, scatter_row, jnp.zeros((block_rows, BLOCK, feature_width), jnp.float32))
    features_grad = self_term + scattered.reshape(NODES, feature_width)
    scaling = float(NODES) ** -0.5
    self_grad = jnp.dot(features.T, masked_grad, preferred_element_type=jnp.float32) * scaling
    neighbor_grad = jnp.dot(aggregate.T, masked_grad, preferred_element_type=jnp.float32) * scaling
    return (features_grad, self_grad, neighbor_grad)
```

```python
import jax
import jax.numpy as jnp
from jax import lax
from jax.experimental import pallas as pl
from jax.experimental.pallas import tpu as pltpu
from jax.sharding import PartitionSpec as P

BF = jnp.bfloat16
F32 = jnp.float32
VMEM_LIMIT = 48 * 2**20


def shifted(array, axis, by):
    size = lax.axis_size(axis)
    return lax.ppermute(array, axis, [(i, (i + by) % size) for i in range(size)])


def sparse_kernel(
    pos_ref, w_hbm, g_hbm, m_hbm, gout_ref, low_ref, own_ref, up_ref,
    acc_ref, w_ref, g_ref, m_ref, wsem, gsem, msem,
):
    blocks, slots, size, _ = w_hbm.shape
    chunks = gsem.shape[0]
    per = blocks // chunks
    rows = per * size

    def gcopy(i):
        part = pl.ds(i * rows, rows)
        return pltpu.make_async_copy(g_hbm.at[part], g_ref.at[part], gsem.at[i])

    def mcopy(i):
        part = pl.ds(i * rows, rows)
        return pltpu.make_async_copy(m_hbm.at[part], m_ref.at[part], msem.at[i])

    def wcopy(b):
        return pltpu.make_async_copy(w_hbm.at[b], w_ref.at[b], wsem.at[b])

    for i in range(chunks):
        gcopy(i).start()
        mcopy(i).start()
        for b in range(i * per, (i + 1) * per):
            wcopy(b).start()
    acc_ref[...] = jnp.zeros_like(acc_ref)

    @pl.loop(0, blocks)
    def _(b):
        @pl.when(lax.rem(b, per) == 0)
        def _():
            i = lax.div(b, per)
            gcopy(i).wait()
            mcopy(i).wait()

        wcopy(b).wait()
        part = pl.ds(pl.multiple_of(b * size, size), size)
        grad = g_ref[part, :] * m_ref[part, :].astype(BF)
        gout_ref[part, :] = grad
        grad_t = grad.T
        for s in range(0, slots, 2):
            pair = jnp.concatenate([w_ref[b, s], w_ref[b, s + 1]], axis=1)
            terms = jnp.dot(grad_t, pair, preferred_element_type=F32)
            acc_ref[pos_ref[b * slots + s]] += terms[:, :size]
            acc_ref[pos_ref[b * slots + s + 1]] += terms[:, size:]

    low_ref[...] = acc_ref[0:blocks].astype(BF)
    own_ref[...] = acc_ref[blocks : 2 * blocks]
    up_ref[...] = acc_ref[2 * blocks : 3 * blocks].astype(BF)


def sparse_pass(destinations, weights, grad, mask):
    blocks, slots, size, _ = weights.shape
    rows, width = grad.shape
    chunks = 4
    vmem = pl.BlockSpec(memory_space=pltpu.VMEM)
    hbm = pl.BlockSpec(memory_space=pltpu.HBM)
    smem = pl.BlockSpec(memory_space=pltpu.SMEM)
    side = (blocks, width, size)
    return pl.pallas_call(
        sparse_kernel,
        in_specs=[smem, hbm, hbm, hbm],
        out_specs=[vmem] * 4,
        out_shape=[
            jax.ShapeDtypeStruct((rows, width), BF),
            jax.ShapeDtypeStruct(side, BF),
            jax.ShapeDtypeStruct(side, F32),
            jax.ShapeDtypeStruct(side, BF),
        ],
        scratch_shapes=[
            pltpu.VMEM((3 * blocks + 1, width, size), F32),
            pltpu.VMEM(weights.shape, BF),
            pltpu.VMEM((rows, width), BF),
            pltpu.VMEM((rows, width), jnp.int32),
            pltpu.SemaphoreType.DMA((blocks,)),
            pltpu.SemaphoreType.DMA((chunks,)),
            pltpu.SemaphoreType.DMA((chunks,)),
        ],
        compiler_params=pltpu.CompilerParams(vmem_limit_bytes=VMEM_LIMIT),
        cost_estimate=pl.CostEstimate(
            flops=2 * blocks * slots * size * size * width,
            bytes_accessed=16 * 2**20,
            transcendentals=0,
        ),
    )(destinations, weights, grad, mask)


def pack_kernel(feat_ref, own_ref, up_ref, low_ref, fown_ref, foth_ref, out_ref, hi_ref, lo_ref):
    blocks, width, size = own_ref.shape
    parts = out_ref.shape[0]
    per = blocks // parts
    for b in range(blocks):
        total = own_ref[b] + up_ref[b].astype(F32) + low_ref[b].astype(F32)
        hi = total.astype(BF)
        out_ref[b // per, (b % per) * width : (b % per + 1) * width, :] = hi
        hi_ref[:, b * size : (b + 1) * size] = hi
        lo_ref[:, b * size : (b + 1) * size] = (total - hi.astype(F32)).astype(BF)
    products = []
    for f_ref in (fown_ref, foth_ref):
        products.append(
            jnp.dot(hi_ref[...], f_ref[...], preferred_element_type=F32)
            + jnp.dot(lo_ref[...], f_ref[...], preferred_element_type=F32)
        )
    first = feat_ref[0] == 0
    rows = width // parts
    base = per * width
    for f in range(2):
        value = jnp.where(first, products[f], products[1 - f])
        hi = value.astype(BF)
        lo = (value - hi.astype(F32)).astype(BF)
        for level, piece in enumerate((hi, lo)):
            for c in range(width // size):
                at = base + ((f * 2 + level) * (width // size) + c) * rows
                for p in range(parts):
                    out_ref[p, at : at + rows, :] = piece[
                        p * rows : (p + 1) * rows, c * size : (c + 1) * size
                    ]


def pack(feat_index, own, up, low, features, features_other, parts):
    blocks, width, size = own.shape
    vmem = pl.BlockSpec(memory_space=pltpu.VMEM)
    smem = pl.BlockSpec(memory_space=pltpu.SMEM)
    rows = (blocks // parts) * width + 4 * (width // size) * (width // parts)
    return pl.pallas_call(
        pack_kernel,
        in_specs=[smem] + [vmem] * 5,
        out_specs=vmem,
        out_shape=jax.ShapeDtypeStruct((parts, rows, size), BF),
        scratch_shapes=[
            pltpu.VMEM((width, blocks * size), BF),
            pltpu.VMEM((width, blocks * size), BF),
        ],
        compiler_params=pltpu.CompilerParams(vmem_limit_bytes=VMEM_LIMIT),
    )(feat_index, own, up, low, features, features_other)


def finish_kernel(own_ref, oth_ref, wown_ref, woth_ref, self_ref, out_ref):
    per, width, size = own_ref.shape
    for b in range(per):
        total = self_ref[b * size : (b + 1) * size, :]
        for h_ref, w_ref in ((own_ref, wown_ref), (oth_ref, woth_ref)):
            h = h_ref[b].T
            hi = h.astype(BF)
            lo = (h - hi.astype(F32)).astype(BF)
            for piece in (hi, lo):
                total += lax.dot_general(
                    piece, w_ref[...], (((1,), (1,)), ((), ())), preferred_element_type=F32
                )
        out_ref[b * size : (b + 1) * size, :] = total


def finish(h_own, h_other, w_own, w_other, self_term):
    vmem = pl.BlockSpec(memory_space=pltpu.VMEM)
    return pl.pallas_call(
        finish_kernel,
        in_specs=[vmem] * 5,
        out_specs=vmem,
        out_shape=jax.ShapeDtypeStruct(self_term.shape, F32),
        compiler_params=pltpu.CompilerParams(vmem_limit_bytes=VMEM_LIMIT),
    )(h_own, h_other, w_own, w_other, self_term)


def row_sum(piece):
    count = lax.axis_size("row")
    sent = jnp.broadcast_to(piece.astype(BF)[None], (count,) + piece.shape)
    return lax.all_to_all(sent, "row", 0, 0).astype(F32).sum(0)


def collect(piece, scaling):
    reps, feats = lax.axis_size("rep"), lax.axis_size("feat")
    halves, columns, rows, lanes = piece.shape
    sent = jnp.broadcast_to((piece * scaling)[:, None], (halves, reps, columns, rows, lanes))
    sent = sent.reshape(feats * reps, columns, rows, lanes)
    got = lax.all_to_all(sent, ("feat", "rep"), 0, 0)
    return got.transpose(1, 3, 0, 2).reshape(columns * lanes, feats * reps * rows)


def local(
    features,
    grad_out,
    relu_mask,
    block_columns,
    block_count,
    block_weights,
    self_weight,
    neighbor_weight,
):
    row_devices = lax.axis_size("row")
    rep_devices = lax.axis_size("rep")
    row_index = lax.axis_index("row")
    rep_index = lax.axis_index("rep")
    feat_index = lax.axis_index("feat")
    first = feat_index == 0
    local_blocks, slot_width = block_columns.shape
    block_size = block_weights.shape[2]
    row_count, half_width = features.shape
    share_rows = row_count // rep_devices
    share_start = rep_index * share_rows
    scaling = float(row_count * row_devices) ** (-0.5)

    slot_number = rep_index * slot_width + jnp.arange(slot_width, dtype=jnp.int32)
    live_slots = slot_number[None, :] < block_count[:, None]
    relative = (block_columns // local_blocks - row_index) % row_devices
    side = jnp.where(relative == row_devices - 1, 0, jnp.where(relative == 0, 1, 2))
    destinations = jnp.where(
        live_slots, side * local_blocks + block_columns % local_blocks, 3 * local_blocks
    ).reshape(-1)

    features_other = shifted(features, "feat", 1)
    masked_grad, to_lower, own, to_upper = sparse_pass(
        destinations, block_weights, grad_out, relu_mask
    )
    from_upper = shifted(to_lower, "row", -1)
    from_lower = shifted(to_upper, "row", 1)

    lanes = block_size
    chunks = half_width // lanes
    share = half_width // rep_devices

    def self_part(values):
        whole = jnp.einsum("ro,rd->od", masked_grad, values, preferred_element_type=F32)
        mine = lax.dynamic_slice_in_dim(whole, rep_index * share, share, 0)
        return mine.reshape(share, chunks, lanes).transpose(1, 0, 2)

    self_own = self_part(features)
    self_oth = self_part(features_other)
    self_piece = jnp.stack(
        [jnp.where(first, self_own, self_oth), jnp.where(first, self_oth, self_own)]
    )
    self_grad = collect(row_sum(self_piece), scaling)

    grad_rows = lax.dynamic_slice_in_dim(masked_grad, share_start, share_rows, 0)
    grad_rows_other = shifted(grad_rows, "feat", 1)

    def halves(weight):
        left, right = weight[:, :half_width], weight[:, half_width:]
        return jnp.where(first, left, right), jnp.where(first, right, left)

    self_w_own, self_w_oth = halves(self_weight)
    neighbor_w_own, neighbor_w_oth = halves(neighbor_weight)
    self_term = jnp.einsum(
        "ro,do->rd", grad_rows, self_w_own, preferred_element_type=F32
    ) + jnp.einsum("ro,do->rd", grad_rows_other, self_w_oth, preferred_element_type=F32)

    payload = pack(
        feat_index.reshape(1).astype(jnp.int32),
        own, from_upper, from_lower, features, features_other, rep_devices,
    )
    got = lax.all_to_all(payload, "rep", 0, 0).astype(F32).sum(0)
    share_blocks = local_blocks // rep_devices
    edge = share_blocks * half_width
    h_own = got[:edge].reshape(share_blocks, half_width, lanes)
    h_other = shifted(h_own, "feat", 1)
    features_grad = finish(h_own, h_other, neighbor_w_own, neighbor_w_oth, self_term)

    neighbor_piece = got[edge:].reshape(2, 2, chunks, share, lanes).sum(1)
    neighbor_grad = collect(row_sum(neighbor_piece), scaling)
    return (features_grad, self_grad, neighbor_grad)


def solution(mesh):
    return jax.shard_map(
        local,
        mesh=mesh,
        in_specs=(
            P("row", "feat"),
            P("row", "feat"),
            P("row", "feat"),
            P("row", "rep"),
            P("row"),
            P("row", "rep", None, None),
            P("feat", None),
            P("feat", None),
        ),
        out_specs=(P(("row", "rep"), "feat"), P("feat", None), P("feat", None)),
        check_vma=False,
    )
```

```python
import jax
import jax.numpy as jnp
from jax import lax
from jax.experimental import pallas as pl
from jax.experimental.pallas import tpu as pltpu
from jax.sharding import PartitionSpec as P

BF = jnp.bfloat16
F32 = jnp.float32
VMEM_LIMIT = 48 * 2**20


def shifted(array, axis, by):
    size = lax.axis_size(axis)
    return lax.ppermute(array, axis, [(i, (i + by) % size) for i in range(size)])


def sparse_kernel(
    pos_ref, w_hbm, g_ref, out_ref, acc_ref, w_ref, wsem
):
    blocks, slots, size, _ = w_hbm.shape

    def wcopy(b):
        return pltpu.make_async_copy(w_hbm.at[b], w_ref.at[b], wsem.at[b])

    for b in range(blocks):
        wcopy(b).start()
    acc_ref[...] = jnp.zeros_like(acc_ref)

    @pl.loop(0, blocks)
    def _(b):
        wcopy(b).wait()
        part = pl.ds(pl.multiple_of(b * size, size), size)
        grad_t = g_ref[part, :].T
        for s in range(0, slots, 2):
            pair = jnp.concatenate([w_ref[b, s], w_ref[b, s + 1]], axis=1)
            terms = jnp.dot(grad_t, pair, preferred_element_type=F32)
            acc_ref[pos_ref[b * slots + s]] += terms[:, :size]
            acc_ref[pos_ref[b * slots + s + 1]] += terms[:, size:]

    width = g_ref.shape[1]
    pieces = blocks // out_ref.shape[0]
    for side in range(3):
        for b in range(blocks):
            at = (side * pieces + b % pieces) * width
            out_ref[b // pieces, at : at + width, :] = acc_ref[side * blocks + b].astype(BF)


def sparse_pass(destinations, weights, grad, parts):
    blocks, slots, size, _ = weights.shape
    width = grad.shape[1]
    vmem = pl.BlockSpec(memory_space=pltpu.VMEM)
    hbm = pl.BlockSpec(memory_space=pltpu.HBM)
    smem = pl.BlockSpec(memory_space=pltpu.SMEM)
    pieces = blocks // parts
    return pl.pallas_call(
        sparse_kernel,
        in_specs=[smem, hbm, vmem],
        out_specs=vmem,
        out_shape=jax.ShapeDtypeStruct((parts, 3 * pieces * width, size), BF),
        scratch_shapes=[
            pltpu.VMEM((3 * blocks + 1, width, size), F32),
            pltpu.VMEM(weights.shape, BF),
            pltpu.SemaphoreType.DMA((blocks,)),
        ],
        compiler_params=pltpu.CompilerParams(vmem_limit_bytes=VMEM_LIMIT),
        cost_estimate=pl.CostEstimate(
            flops=2 * blocks * slots * size * size * width,
            bytes_accessed=13 * 2**20,
            transcendentals=0,
        ),
    )(destinations, weights, grad)


def product_kernel(feat_ref, sums_ref, *refs):
    f_refs, out_ref, h_ref = refs[:6], refs[6], refs[7]
    parts, depth, size = sums_ref.shape
    width = f_refs[0].shape[1]
    pieces = depth // (3 * width)
    for side in range(3):
        for b in range(parts * pieces):
            at = (side * pieces + b % pieces) * width
            h_ref[side, :, b * size : (b + 1) * size] = sums_ref[b // pieces, at : at + width, :]
    products = []
    for which in range(2):
        total = jnp.zeros((width, width), F32)
        for side in range(3):
            total += jnp.dot(
                h_ref[side], f_refs[side * 2 + which][...], preferred_element_type=F32
            )
        products.append(total)
    first = feat_ref[0] == 0
    targets = out_ref.shape[0]
    rows = width // targets
    chunks = width // size
    for f in range(2):
        piece = jnp.where(first, products[f], products[1 - f]).astype(BF)
        for c in range(chunks):
            at = (f * chunks + c) * rows
            for t in range(targets):
                out_ref[t, at : at + rows, :] = piece[
                    t * rows : (t + 1) * rows, c * size : (c + 1) * size
                ]


def product(feat_index, sums, features, targets):
    size = sums.shape[2]
    rows, width = features[0].shape
    vmem = pl.BlockSpec(memory_space=pltpu.VMEM)
    smem = pl.BlockSpec(memory_space=pltpu.SMEM)
    depth = 2 * (width // size) * (width // targets)
    return pl.pallas_call(
        product_kernel,
        in_specs=[smem] + [vmem] * (1 + len(features)),
        out_specs=vmem,
        out_shape=jax.ShapeDtypeStruct((targets, depth, size), BF),
        scratch_shapes=[pltpu.VMEM((3, width, rows), BF)],
        compiler_params=pltpu.CompilerParams(vmem_limit_bytes=VMEM_LIMIT),
        cost_estimate=pl.CostEstimate(
            flops=90 * rows * width * width, bytes_accessed=10 * 2**20, transcendentals=0
        ),
    )(feat_index, sums, *features)


def finish_kernel(own_ref, oth_ref, wown_ref, woth_ref, self_ref, out_ref):
    per, width, size = own_ref.shape
    for b in range(per):
        total = self_ref[b * size : (b + 1) * size, :]
        for h_ref, w_ref in ((own_ref, wown_ref), (oth_ref, woth_ref)):
            h = h_ref[b].T
            hi = h.astype(BF)
            lo = (h - hi.astype(F32)).astype(BF)
            for piece in (hi, lo):
                total += lax.dot_general(
                    piece, w_ref[...], (((1,), (1,)), ((), ())), preferred_element_type=F32
                )
        out_ref[b * size : (b + 1) * size, :] = total


def finish(h_own, h_other, w_own, w_other, self_term):
    vmem = pl.BlockSpec(memory_space=pltpu.VMEM)
    return pl.pallas_call(
        finish_kernel,
        in_specs=[vmem] * 5,
        out_specs=vmem,
        out_shape=jax.ShapeDtypeStruct(self_term.shape, F32),
        compiler_params=pltpu.CompilerParams(vmem_limit_bytes=VMEM_LIMIT),
    )(h_own, h_other, w_own, w_other, self_term)


def exchanged(value, step):
    count = lax.axis_size("row")
    return value + lax.ppermute(value, "row", [(i, i ^ step) for i in range(count)])


def whole(pieces, scaling):
    count, columns, rows, lanes = pieces.shape
    scaled = pieces.astype(F32) * scaling
    return scaled.transpose(1, 3, 0, 2).reshape(columns * lanes, count * rows)


def collect(piece):
    rows, feats = lax.axis_size("row"), lax.axis_size("feat")
    sent = jnp.broadcast_to(piece[:, None], (feats, rows) + piece.shape[1:])
    sent = sent.reshape((feats * rows,) + piece.shape[1:])
    return lax.all_to_all(sent, ("feat", "row"), 0, 0)


def local(
    features,
    grad_out,
    relu_mask,
    block_columns,
    block_count,
    block_weights,
    self_weight,
    neighbor_weight,
):
    row_devices = lax.axis_size("row")
    rep_devices = lax.axis_size("rep")
    row_index = lax.axis_index("row")
    rep_index = lax.axis_index("rep")
    feat_index = lax.axis_index("feat")
    first = feat_index == 0
    local_blocks, slot_width = block_columns.shape
    block_size = block_weights.shape[2]
    row_count, half_width = features.shape
    share_rows = row_count // rep_devices
    share_start = rep_index * share_rows
    scaling = float(row_count * row_devices) ** (-0.5)

    slot_number = rep_index * slot_width + jnp.arange(slot_width, dtype=jnp.int32)
    live_slots = slot_number[None, :] < block_count[:, None]
    relative = (block_columns // local_blocks - row_index) % row_devices
    side = jnp.where(relative == row_devices - 1, 0, jnp.where(relative == 0, 1, 2))
    destinations = jnp.where(
        live_slots, side * local_blocks + block_columns % local_blocks, 3 * local_blocks
    ).reshape(-1)

    before, after = shifted(features, "row", 1), shifted(features, "row", -1)
    features_other = shifted(features, "feat", 1)
    masked_grad = grad_out * relu_mask.astype(BF)

    lanes = block_size
    chunks = half_width // lanes
    share = half_width // rep_devices

    def self_part(values):
        whole = jnp.einsum("ro,rd->od", masked_grad, values, preferred_element_type=F32)
        mine = lax.dynamic_slice_in_dim(whole, rep_index * share, share, 0)
        return mine.reshape(share, chunks, lanes).transpose(1, 0, 2)

    self_own = self_part(features)
    self_oth = self_part(features_other)
    self_piece = jnp.stack(
        [jnp.where(first, self_own, self_oth), jnp.where(first, self_oth, self_own)]
    )
    self_piece, grad_values = lax.optimization_barrier((self_piece, masked_grad))
    sums = sparse_pass(destinations, block_weights, grad_values, rep_devices)
    sums_got = lax.all_to_all(sums, "rep", 0, 0)
    before, after, sums = lax.optimization_barrier((before, after, sums))
    extended = []
    for rows, other in ((before, None), (features, features_other), (after, None)):
        extended += [rows, shifted(rows, "feat", 1) if other is None else other]

    grad_rows = lax.dynamic_slice_in_dim(masked_grad, share_start, share_rows, 0)
    grad_rows_other = shifted(grad_rows, "feat", 1)

    def halves(weight):
        left, right = weight[:, :half_width], weight[:, half_width:]
        return jnp.where(first, left, right), jnp.where(first, right, left)

    self_w_own, self_w_oth = halves(self_weight)
    neighbor_w_own, neighbor_w_oth = halves(neighbor_weight)
    self_term = jnp.einsum(
        "ro,do->rd", grad_rows, self_w_own, preferred_element_type=F32
    ) + jnp.einsum("ro,do->rd", grad_rows_other, self_w_oth, preferred_element_type=F32)

    products = product(feat_index.reshape(1).astype(jnp.int32), sums, extended, row_devices)
    self_sum, products = lax.optimization_barrier((self_piece, products))
    step = 1
    while 2 * step < row_devices:
        self_sum = exchanged(self_sum, step)
        step *= 2
    products, sums_got, self_sum = lax.optimization_barrier((products, sums_got, self_sum))
    products_got = lax.all_to_all(products, "row", 0, 0)
    if step < row_devices:
        self_sum = exchanged(self_sum, step)

    edge = (local_blocks // rep_devices) * half_width
    summed = sums_got.astype(F32).sum(0)
    from_upper = shifted(summed[:edge], "row", -1)
    from_lower = shifted(summed[2 * edge :], "row", 1)

    product_sum = products_got.astype(F32).sum(0)
    product_hi = product_sum.astype(BF)
    product_lo = (product_sum - product_hi.astype(F32)).astype(BF)
    self_rows = self_sum.astype(BF).reshape(-1, lanes)
    to_all = jnp.concatenate([product_hi, product_lo, self_rows])
    got = lax.all_to_all(
        jnp.broadcast_to(to_all[None], (rep_devices,) + to_all.shape), "rep", 0, 0
    )
    middle = product_sum.shape[0]
    neighbor_piece = (got[:, :middle].astype(F32) + got[:, middle : 2 * middle].astype(F32)).sum(0)
    neighbor_piece = neighbor_piece.reshape(2, chunks, -1, lanes)
    neighbor_grad = whole(collect(neighbor_piece), scaling)

    h_own = (summed[edge : 2 * edge] + from_upper + from_lower).reshape(-1, half_width, lanes)
    h_other = shifted(h_own, "feat", 1)
    features_grad = finish(h_own, h_other, neighbor_w_own, neighbor_w_oth, self_term)

    self_pieces = got[:, 2 * middle :].reshape((rep_devices,) + self_sum.shape)
    keep = jnp.where(first, self_pieces[:, 0], self_pieces[:, 1])
    send = jnp.where(first, self_pieces[:, 1], self_pieces[:, 0])
    came = shifted(send, "feat", 1)
    self_grad = whole(
        jnp.concatenate([jnp.where(first, keep, came), jnp.where(first, came, keep)]), scaling
    )
    return (features_grad, self_grad, neighbor_grad)


def solution(mesh):
    return jax.shard_map(
        local,
        mesh=mesh,
        in_specs=(
            P("row", "feat"),
            P("row", "feat"),
            P("row", "feat"),
            P("row", "rep"),
            P("row"),
            P("row", "rep", None, None),
            P("feat", None),
            P("feat", None),
        ),
        out_specs=(P(("row", "rep"), "feat"), P("feat", None), P("feat", None)),
        check_vma=False,
    )
```

```python
import jax
import jax.numpy as jnp
from jax import lax
from jax.experimental import pallas as pl
from jax.experimental.pallas import tpu as pltpu
from jax.sharding import PartitionSpec as P

BF = jnp.bfloat16
F32 = jnp.float32
VMEM_LIMIT = 48 * 2**20


def shifted(array, axis, by):
    size = lax.axis_size(axis)
    return lax.ppermute(array, axis, [(i, (i + by) % size) for i in range(size)])


def sparse_kernel(
    pos_ref, w_hbm, g_ref, sides_ref, own_ref, acc_ref, w_ref, wsem
):
    blocks, slots, size, _ = w_hbm.shape

    def wcopy(b):
        return pltpu.make_async_copy(w_hbm.at[b], w_ref.at[b], wsem.at[b])

    for b in range(blocks):
        wcopy(b).start()
    acc_ref[...] = jnp.zeros_like(acc_ref)

    @pl.loop(0, blocks)
    def _(b):
        wcopy(b).wait()
        part = pl.ds(pl.multiple_of(b * size, size), size)
        grad_t = g_ref[part, :].T
        for s in range(0, slots, 2):
            pair = jnp.concatenate([w_ref[b, s], w_ref[b, s + 1]], axis=1)
            terms = jnp.dot(grad_t, pair, preferred_element_type=F32)
            acc_ref[pos_ref[b * slots + s]] += terms[:, :size]
            acc_ref[pos_ref[b * slots + s + 1]] += terms[:, size:]

    width = g_ref.shape[1]
    pieces = blocks // own_ref.shape[0]
    for b in range(blocks):
        at = (b % pieces) * width
        for side, ref, to in ((0, sides_ref, at), (1, own_ref, at), (2, sides_ref, pieces * width + at)):
            ref[b // pieces, to : to + width, :] = acc_ref[side * blocks + b].astype(BF)


def sparse_pass(destinations, weights, grad, parts):
    blocks, slots, size, _ = weights.shape
    width = grad.shape[1]
    vmem = pl.BlockSpec(memory_space=pltpu.VMEM)
    hbm = pl.BlockSpec(memory_space=pltpu.HBM)
    smem = pl.BlockSpec(memory_space=pltpu.SMEM)
    pieces = blocks // parts
    return pl.pallas_call(
        sparse_kernel,
        in_specs=[smem, hbm, vmem],
        out_specs=[vmem] * 2,
        out_shape=[
            jax.ShapeDtypeStruct((parts, 2 * pieces * width, size), BF),
            jax.ShapeDtypeStruct((parts, pieces * width, size), BF),
        ],
        scratch_shapes=[
            pltpu.VMEM((3 * blocks + 1, width, size), F32),
            pltpu.VMEM(weights.shape, BF),
            pltpu.SemaphoreType.DMA((blocks,)),
        ],
        compiler_params=pltpu.CompilerParams(vmem_limit_bytes=VMEM_LIMIT),
        cost_estimate=pl.CostEstimate(
            flops=2 * blocks * slots * size * size * width,
            bytes_accessed=13 * 2**20,
            transcendentals=0,
        ),
    )(destinations, weights, grad)


def product_kernel(feat_ref, own_hbm, sides_hbm, *refs):
    f_hbm, (out_ref, own_ref, sides_ref, h_ref, f_ref, sem) = refs[:6], refs[6:]
    ends = [(own_hbm, own_ref), (sides_hbm, sides_ref)]
    ends += [(f_hbm[i], f_ref.at[i]) for i in range(6)]
    copies = [pltpu.make_async_copy(a, b, sem.at[i]) for i, (a, b) in enumerate(ends)]
    for copy in copies:
        copy.start()
    parts, edge, size = own_ref.shape
    width = f_ref.shape[2]
    pieces = edge // width
    copies[0].wait()
    copies[1].wait()
    for side, ref, base in ((0, sides_ref, 0), (1, own_ref, 0), (2, sides_ref, edge)):
        for b in range(parts * pieces):
            at = base + (b % pieces) * width
            h_ref[side, :, b * size : (b + 1) * size] = ref[b // pieces, at : at + width, :]
    for copy in copies[2:]:
        copy.wait()
    products = []
    for which in range(2):
        total = jnp.zeros((width, width), F32)
        for side in range(3):
            total += jnp.dot(
                h_ref[side], f_ref[side * 2 + which], preferred_element_type=F32
            )
        products.append(total)
    first = feat_ref[0] == 0
    targets = out_ref.shape[0]
    rows = width // targets
    chunks = width // size
    for f in range(2):
        piece = jnp.where(first, products[f], products[1 - f]).astype(BF)
        for c in range(chunks):
            at = (f * chunks + c) * rows
            for t in range(targets):
                out_ref[t, at : at + rows, :] = piece[
                    t * rows : (t + 1) * rows, c * size : (c + 1) * size
                ]


def product(feat_index, own, sides, features, targets):
    size = own.shape[2]
    rows, width = features[0].shape
    vmem = pl.BlockSpec(memory_space=pltpu.VMEM)
    smem = pl.BlockSpec(memory_space=pltpu.SMEM)
    hbm = pl.BlockSpec(memory_space=pltpu.HBM)
    depth = 2 * (width // size) * (width // targets)
    return pl.pallas_call(
        product_kernel,
        in_specs=[smem] + [hbm] * (2 + len(features)),
        out_specs=vmem,
        out_shape=jax.ShapeDtypeStruct((targets, depth, size), BF),
        scratch_shapes=[
            pltpu.VMEM(own.shape, BF),
            pltpu.VMEM(sides.shape, BF),
            pltpu.VMEM((3, width, rows), BF),
            pltpu.VMEM((len(features), rows, width), BF),
            pltpu.SemaphoreType.DMA((2 + len(features),)),
        ],
        compiler_params=pltpu.CompilerParams(vmem_limit_bytes=VMEM_LIMIT),
        cost_estimate=pl.CostEstimate(
            flops=12 * rows * width * width, bytes_accessed=10 * 2**20, transcendentals=0
        ),
    )(feat_index, own, sides, *features)


def finish_kernel(own_ref, oth_ref, wown_ref, woth_ref, self_ref, out_ref):
    per, width, size = own_ref.shape
    for b in range(per):
        total = self_ref[b * size : (b + 1) * size, :]
        for h_ref, w_ref in ((own_ref, wown_ref), (oth_ref, woth_ref)):
            h = h_ref[b].T
            hi = h.astype(BF)
            lo = (h - hi.astype(F32)).astype(BF)
            for piece in (hi, lo):
                total += lax.dot_general(
                    piece, w_ref[...], (((1,), (1,)), ((), ())), preferred_element_type=F32
                )
        out_ref[b * size : (b + 1) * size, :] = total


def finish(h_own, h_other, w_own, w_other, self_term):
    vmem = pl.BlockSpec(memory_space=pltpu.VMEM)
    return pl.pallas_call(
        finish_kernel,
        in_specs=[vmem] * 5,
        out_specs=vmem,
        out_shape=jax.ShapeDtypeStruct(self_term.shape, F32),
        compiler_params=pltpu.CompilerParams(vmem_limit_bytes=VMEM_LIMIT),
    )(h_own, h_other, w_own, w_other, self_term)


def exchanged(value, step):
    count = lax.axis_size("row")
    return value + lax.ppermute(value, "row", [(i, i ^ step) for i in range(count)])


def whole(pieces, scaling):
    count, columns, rows, lanes = pieces.shape
    scaled = pieces.astype(F32) * scaling
    return scaled.transpose(1, 3, 0, 2).reshape(columns * lanes, count * rows)


def collect(piece):
    rows, feats = lax.axis_size("row"), lax.axis_size("feat")
    sent = jnp.broadcast_to(piece[:, None], (feats, rows) + piece.shape[1:])
    sent = sent.reshape((feats * rows,) + piece.shape[1:])
    return lax.all_to_all(sent, ("feat", "row"), 0, 0)


def local(
    features,
    grad_out,
    relu_mask,
    block_columns,
    block_count,
    block_weights,
    self_weight,
    neighbor_weight,
):
    row_devices = lax.axis_size("row")
    rep_devices = lax.axis_size("rep")
    row_index = lax.axis_index("row")
    rep_index = lax.axis_index("rep")
    feat_index = lax.axis_index("feat")
    first = feat_index == 0
    local_blocks, slot_width = block_columns.shape
    block_size = block_weights.shape[2]
    row_count, half_width = features.shape
    share_rows = row_count // rep_devices
    share_start = rep_index * share_rows
    scaling = float(row_count * row_devices) ** (-0.5)

    slot_number = rep_index * slot_width + jnp.arange(slot_width, dtype=jnp.int32)
    live_slots = slot_number[None, :] < block_count[:, None]
    relative = (block_columns // local_blocks - row_index) % row_devices
    side = jnp.where(relative == row_devices - 1, 0, jnp.where(relative == 0, 1, 2))
    destinations = jnp.where(
        live_slots, side * local_blocks + block_columns % local_blocks, 3 * local_blocks
    ).reshape(-1)

    before, after = shifted(features, "row", 1), shifted(features, "row", -1)
    features_other = shifted(features, "feat", 1)
    masked_grad = grad_out * relu_mask.astype(BF)

    lanes = block_size
    chunks = half_width // lanes
    share = half_width // rep_devices

    def self_part(values):
        whole = jnp.einsum("ro,rd->od", masked_grad, values, preferred_element_type=F32)
        mine = lax.dynamic_slice_in_dim(whole, rep_index * share, share, 0)
        return mine.reshape(share, chunks, lanes).transpose(1, 0, 2)

    self_own = self_part(features)
    self_oth = self_part(features_other)
    self_piece = jnp.stack(
        [jnp.where(first, self_own, self_oth), jnp.where(first, self_oth, self_own)]
    )
    self_piece, grad_values = lax.optimization_barrier((self_piece, masked_grad))
    sides, own = sparse_pass(destinations, block_weights, grad_values, rep_devices)
    sides_got = lax.all_to_all(sides, "rep", 0, 0)
    before, after, own = lax.optimization_barrier((before, after, own))
    self_sum, step = self_piece, 1
    while 4 * step < row_devices:
        self_sum = exchanged(self_sum, step)
        step *= 2
    self_sum, own = lax.optimization_barrier((self_sum, own))
    if 2 * step < row_devices:
        self_sum = exchanged(self_sum, step)
        step *= 2
    extended = []
    for rows, other in ((before, None), (features, features_other), (after, None)):
        extended += [rows, shifted(rows, "feat", 1) if other is None else other]

    grad_rows = lax.dynamic_slice_in_dim(masked_grad, share_start, share_rows, 0)
    grad_rows_other = shifted(grad_rows, "feat", 1)

    def halves(weight):
        left, right = weight[:, :half_width], weight[:, half_width:]
        return jnp.where(first, left, right), jnp.where(first, right, left)

    self_w_own, self_w_oth = halves(self_weight)
    neighbor_w_own, neighbor_w_oth = halves(neighbor_weight)
    self_term = jnp.einsum(
        "ro,do->rd", grad_rows, self_w_own, preferred_element_type=F32
    ) + jnp.einsum("ro,do->rd", grad_rows_other, self_w_oth, preferred_element_type=F32)

    products = product(
        feat_index.reshape(1).astype(jnp.int32), own, sides, extended, row_devices
    )
    products, sides_got, self_sum = lax.optimization_barrier((products, sides_got, self_sum))
    products_got = lax.all_to_all(products, "row", 0, 0)
    if step < row_devices:
        self_sum = exchanged(self_sum, step)

    edge = (local_blocks // rep_devices) * half_width
    sides_sum = sides_got.astype(F32).sum(0).astype(BF)
    from_upper = shifted(sides_sum[:edge], "row", -1)
    from_lower = shifted(sides_sum[edge:], "row", 1)

    product_sum = products_got.astype(F32).sum(0)
    product_hi = lax.reduce_precision(product_sum, 8, 7)
    product_lo = (product_sum - product_hi).astype(BF)
    self_rows = self_sum.astype(BF).reshape(-1, lanes)
    to_all = jnp.concatenate([product_hi.astype(BF), product_lo, self_rows])
    to_all = jnp.broadcast_to(to_all[None], (rep_devices,) + to_all.shape)
    got = lax.all_to_all(jnp.concatenate([own, to_all], axis=1), "rep", 0, 0)
    middle = edge + product_sum.shape[0]
    end = middle + product_sum.shape[0]
    neighbor_piece = (got[:, edge:middle].astype(F32) + got[:, middle:end].astype(F32)).sum(0)
    neighbor_piece = neighbor_piece.reshape(2, chunks, -1, lanes)
    neighbor_grad = whole(collect(neighbor_piece), scaling)

    summed = got[:, :edge].astype(F32).sum(0)
    h_own = summed + from_upper.astype(F32) + from_lower.astype(F32)
    h_own = h_own.reshape(-1, half_width, lanes)
    h_other = shifted(h_own, "feat", 1)
    features_grad = finish(h_own, h_other, neighbor_w_own, neighbor_w_oth, self_term)

    self_pieces = got[:, end:].reshape((rep_devices,) + self_sum.shape)
    keep = jnp.where(first, self_pieces[:, 0], self_pieces[:, 1])
    send = jnp.where(first, self_pieces[:, 1], self_pieces[:, 0])
    came = shifted(send, "feat", 1)
    self_grad = whole(
        jnp.concatenate([jnp.where(first, keep, came), jnp.where(first, came, keep)]), scaling
    )
    return (features_grad, self_grad, neighbor_grad)


def solution(mesh):
    return jax.shard_map(
        local,
        mesh=mesh,
        in_specs=(
            P("row", "feat"),
            P("row", "feat"),
            P("row", "feat"),
            P("row", "rep"),
            P("row"),
            P("row", "rep", None, None),
            P("feat", None),
            P("feat", None),
        ),
        out_specs=(P(("row", "rep"), "feat"), P("feat", None), P("feat", None)),
        check_vma=False,
    )
```

```python
import jax
import jax.numpy as jnp
from jax import lax
from jax.experimental import pallas as pl
from jax.experimental.pallas import tpu as pltpu
from jax.sharding import PartitionSpec as P

BF = jnp.bfloat16
F32 = jnp.float32
VMEM_LIMIT = 48 * 2**20


def shifted(array, axis, by):
    size = lax.axis_size(axis)
    return lax.ppermute(array, axis, [(i, (i + by) % size) for i in range(size)])


def sparse_kernel(
    pos_ref, w_hbm, g_ref, sides_ref, own_ref, acc_ref, w_ref, wsem
):
    blocks, slots, size, _ = w_hbm.shape

    def wcopy(b):
        return pltpu.make_async_copy(w_hbm.at[b], w_ref.at[b], wsem.at[b])

    for b in range(blocks):
        wcopy(b).start()
    acc_ref[...] = jnp.zeros_like(acc_ref)

    @pl.loop(0, blocks)
    def _(b):
        wcopy(b).wait()
        part = pl.ds(pl.multiple_of(b * size, size), size)
        grad_t = g_ref[part, :].T
        for s in range(0, slots, 2):
            pair = jnp.concatenate([w_ref[b, s], w_ref[b, s + 1]], axis=1)
            terms = jnp.dot(grad_t, pair, preferred_element_type=F32)
            acc_ref[pos_ref[b * slots + s]] += terms[:, :size]
            acc_ref[pos_ref[b * slots + s + 1]] += terms[:, size:]

    width = g_ref.shape[1]
    pieces = blocks // own_ref.shape[0]
    for b in range(blocks):
        at = (b % pieces) * width
        for side, ref, to in ((0, sides_ref, at), (1, own_ref, at), (2, sides_ref, pieces * width + at)):
            ref[b // pieces, to : to + width, :] = acc_ref[side * blocks + b].astype(BF)


def sparse_pass(destinations, weights, grad, parts):
    blocks, slots, size, _ = weights.shape
    width = grad.shape[1]
    vmem = pl.BlockSpec(memory_space=pltpu.VMEM)
    hbm = pl.BlockSpec(memory_space=pltpu.HBM)
    smem = pl.BlockSpec(memory_space=pltpu.SMEM)
    pieces = blocks // parts
    return pl.pallas_call(
        sparse_kernel,
        in_specs=[smem, hbm, vmem],
        out_specs=[vmem] * 2,
        out_shape=[
            jax.ShapeDtypeStruct((parts, 2 * pieces * width, size), BF),
            jax.ShapeDtypeStruct((parts, pieces * width, size), BF),
        ],
        scratch_shapes=[
            pltpu.VMEM((3 * blocks + 1, width, size), F32),
            pltpu.VMEM(weights.shape, BF),
            pltpu.SemaphoreType.DMA((blocks,)),
        ],
        compiler_params=pltpu.CompilerParams(vmem_limit_bytes=VMEM_LIMIT),
        cost_estimate=pl.CostEstimate(
            flops=2 * blocks * slots * size * size * width,
            bytes_accessed=13 * 2**20,
            transcendentals=0,
        ),
    )(destinations, weights, grad)


def product_kernel(feat_ref, own_hbm, sides_hbm, *refs):
    f_hbm, (out_ref, own_ref, sides_ref, h_ref, f_ref, sem) = refs[:6], refs[6:]
    ends = [(own_hbm, own_ref), (sides_hbm, sides_ref)]
    ends += [(f_hbm[i], f_ref.at[i]) for i in range(6)]
    copies = [pltpu.make_async_copy(a, b, sem.at[i]) for i, (a, b) in enumerate(ends)]
    for copy in copies:
        copy.start()
    parts, edge, size = own_ref.shape
    width = f_ref.shape[2]
    pieces = edge // width
    copies[0].wait()
    copies[1].wait()
    for side, ref, base in ((0, sides_ref, 0), (1, own_ref, 0), (2, sides_ref, edge)):
        for b in range(parts * pieces):
            at = base + (b % pieces) * width
            h_ref[side, :, b * size : (b + 1) * size] = ref[b // pieces, at : at + width, :]
    for copy in copies[2:]:
        copy.wait()
    products = []
    for which in range(2):
        total = jnp.zeros((width, width), F32)
        for side in range(3):
            total += jnp.dot(
                h_ref[side], f_ref[side * 2 + which], preferred_element_type=F32
            )
        products.append(total)
    first = feat_ref[0] == 0
    targets = out_ref.shape[0]
    rows = width // targets
    chunks = width // size
    for f in range(2):
        value = jnp.where(first, products[f], products[1 - f])
        hi = value.astype(BF)
        lo = (value - hi.astype(F32)).astype(BF)
        for level, piece in enumerate((hi, lo)):
            for c in range(chunks):
                at = ((level * 2 + f) * chunks + c) * rows
                for t in range(targets):
                    out_ref[t, at : at + rows, :] = piece[
                        t * rows : (t + 1) * rows, c * size : (c + 1) * size
                    ]


def product(feat_index, own, sides, features, targets):
    size = own.shape[2]
    rows, width = features[0].shape
    vmem = pl.BlockSpec(memory_space=pltpu.VMEM)
    smem = pl.BlockSpec(memory_space=pltpu.SMEM)
    hbm = pl.BlockSpec(memory_space=pltpu.HBM)
    depth = 4 * (width // size) * (width // targets)
    return pl.pallas_call(
        product_kernel,
        in_specs=[smem] + [hbm] * (2 + len(features)),
        out_specs=vmem,
        out_shape=jax.ShapeDtypeStruct((targets, depth, size), BF),
        scratch_shapes=[
            pltpu.VMEM(own.shape, BF),
            pltpu.VMEM(sides.shape, BF),
            pltpu.VMEM((3, width, rows), BF),
            pltpu.VMEM((len(features), rows, width), BF),
            pltpu.SemaphoreType.DMA((2 + len(features),)),
        ],
        compiler_params=pltpu.CompilerParams(vmem_limit_bytes=VMEM_LIMIT),
        cost_estimate=pl.CostEstimate(
            flops=12 * rows * width * width, bytes_accessed=10 * 2**20, transcendentals=0
        ),
    )(feat_index, own, sides, *features)


def finish_kernel(own_ref, oth_ref, wown_ref, woth_ref, self_ref, out_ref):
    per, width, size = own_ref.shape
    for b in range(per):
        total = self_ref[b * size : (b + 1) * size, :]
        for h_ref, w_ref in ((own_ref, wown_ref), (oth_ref, woth_ref)):
            h = h_ref[b].T
            hi = h.astype(BF)
            lo = (h - hi.astype(F32)).astype(BF)
            for piece in (hi, lo):
                total += lax.dot_general(
                    piece, w_ref[...], (((1,), (1,)), ((), ())), preferred_element_type=F32
                )
        out_ref[b * size : (b + 1) * size, :] = total


def finish(h_own, h_other, w_own, w_other, self_term):
    vmem = pl.BlockSpec(memory_space=pltpu.VMEM)
    return pl.pallas_call(
        finish_kernel,
        in_specs=[vmem] * 5,
        out_specs=vmem,
        out_shape=jax.ShapeDtypeStruct(self_term.shape, F32),
        compiler_params=pltpu.CompilerParams(vmem_limit_bytes=VMEM_LIMIT),
    )(h_own, h_other, w_own, w_other, self_term)


def exchanged(value, step):
    count = lax.axis_size("row")
    return value + lax.ppermute(value, "row", [(i, i ^ step) for i in range(count)])


def whole(pieces, scaling):
    count, columns, rows, lanes = pieces.shape
    scaled = pieces.astype(F32) * scaling
    return scaled.transpose(1, 3, 0, 2).reshape(columns * lanes, count * rows)


def collect(piece):
    rows, feats = lax.axis_size("row"), lax.axis_size("feat")
    sent = jnp.broadcast_to(piece[:, None], (feats, rows) + piece.shape[1:])
    sent = sent.reshape((feats * rows,) + piece.shape[1:])
    return lax.all_to_all(sent, ("feat", "row"), 0, 0)


def local(
    features,
    grad_out,
    relu_mask,
    block_columns,
    block_count,
    block_weights,
    self_weight,
    neighbor_weight,
):
    row_devices = lax.axis_size("row")
    rep_devices = lax.axis_size("rep")
    row_index = lax.axis_index("row")
    rep_index = lax.axis_index("rep")
    feat_index = lax.axis_index("feat")
    first = feat_index == 0
    local_blocks, slot_width = block_columns.shape
    block_size = block_weights.shape[2]
    row_count, half_width = features.shape
    share_rows = row_count // rep_devices
    share_start = rep_index * share_rows
    scaling = float(row_count * row_devices) ** (-0.5)

    slot_number = rep_index * slot_width + jnp.arange(slot_width, dtype=jnp.int32)
    live_slots = slot_number[None, :] < block_count[:, None]
    relative = (block_columns // local_blocks - row_index) % row_devices
    side = jnp.where(relative == row_devices - 1, 0, jnp.where(relative == 0, 1, 2))
    destinations = jnp.where(
        live_slots, side * local_blocks + block_columns % local_blocks, 3 * local_blocks
    ).reshape(-1)

    before, after = shifted(features, "row", 1), shifted(features, "row", -1)
    features_other = shifted(features, "feat", 1)
    masked_grad = grad_out * relu_mask.astype(BF)

    lanes = block_size
    chunks = half_width // lanes
    share = half_width // rep_devices

    def self_part(values):
        whole = jnp.einsum("ro,rd->od", masked_grad, values, preferred_element_type=F32)
        mine = lax.dynamic_slice_in_dim(whole, rep_index * share, share, 0)
        return mine.reshape(share, chunks, lanes).transpose(1, 0, 2)

    self_own = self_part(features)
    self_oth = self_part(features_other)
    self_piece = jnp.stack(
        [jnp.where(first, self_own, self_oth), jnp.where(first, self_oth, self_own)]
    )
    self_piece, grad_values = lax.optimization_barrier((self_piece, masked_grad))
    sides, own = sparse_pass(destinations, block_weights, grad_values, rep_devices)
    sides_got = lax.all_to_all(sides, "rep", 0, 0)
    before, after, own = lax.optimization_barrier((before, after, own))
    self_sum, step = self_piece, 1
    while 4 * step < row_devices:
        self_sum = exchanged(self_sum, step)
        step *= 2
    self_sum, own = lax.optimization_barrier((self_sum, own))
    if 2 * step < row_devices:
        self_sum = exchanged(self_sum, step)
        step *= 2
    extended = []
    for rows, other in ((before, None), (features, features_other), (after, None)):
        extended += [rows, shifted(rows, "feat", 1) if other is None else other]

    grad_rows = lax.dynamic_slice_in_dim(masked_grad, share_start, share_rows, 0)
    grad_rows_other = shifted(grad_rows, "feat", 1)

    def halves(weight):
        left, right = weight[:, :half_width], weight[:, half_width:]
        return jnp.where(first, left, right), jnp.where(first, right, left)

    self_w_own, self_w_oth = halves(self_weight)
    neighbor_w_own, neighbor_w_oth = halves(neighbor_weight)
    self_term = jnp.einsum(
        "ro,do->rd", grad_rows, self_w_own, preferred_element_type=F32
    ) + jnp.einsum("ro,do->rd", grad_rows_other, self_w_oth, preferred_element_type=F32)

    products = product(
        feat_index.reshape(1).astype(jnp.int32), own, sides, extended, row_devices
    )
    products, sides_got, self_sum = lax.optimization_barrier((products, sides_got, self_sum))
    products_got = lax.all_to_all(products, "row", 0, 0)
    if step < row_devices:
        self_sum = exchanged(self_sum, step)

    edge = (local_blocks // rep_devices) * half_width
    sides_sum = sides_got.astype(F32).sum(0).astype(BF)
    from_upper = shifted(sides_sum[:edge], "row", -1)
    from_lower = shifted(sides_sum[edge:], "row", 1)

    product_sum = products_got.astype(F32).sum(0).reshape(2, -1, lanes).sum(0)
    product_hi = lax.reduce_precision(product_sum, 8, 7)
    product_lo = (product_sum - product_hi).astype(BF)
    self_rows = self_sum.astype(BF).reshape(-1, lanes)
    to_all = jnp.concatenate([product_hi.astype(BF), product_lo, self_rows])
    to_all = jnp.broadcast_to(to_all[None], (rep_devices,) + to_all.shape)
    got = lax.all_to_all(jnp.concatenate([own, to_all], axis=1), "rep", 0, 0)
    middle = edge + product_sum.shape[0]
    end = middle + product_sum.shape[0]
    neighbor_piece = (got[:, edge:middle].astype(F32) + got[:, middle:end].astype(F32)).sum(0)
    neighbor_piece = neighbor_piece.reshape(2, chunks, -1, lanes)
    neighbor_grad = whole(collect(neighbor_piece.astype(BF)), scaling)

    summed = got[:, :edge].astype(F32).sum(0)
    h_own = summed + from_upper.astype(F32) + from_lower.astype(F32)
    h_own = h_own.reshape(-1, half_width, lanes)
    h_other = shifted(h_own, "feat", 1)
    features_grad = finish(h_own, h_other, neighbor_w_own, neighbor_w_oth, self_term)

    self_pieces = got[:, end:].reshape((rep_devices,) + self_sum.shape)
    keep = jnp.where(first, self_pieces[:, 0], self_pieces[:, 1])
    send = jnp.where(first, self_pieces[:, 1], self_pieces[:, 0])
    came = shifted(send, "feat", 1)
    self_grad = whole(
        jnp.concatenate([jnp.where(first, keep, came), jnp.where(first, came, keep)]), scaling
    )
    return (features_grad, self_grad, neighbor_grad)


def solution(mesh):
    return jax.shard_map(
        local,
        mesh=mesh,
        in_specs=(
            P("row", "feat"),
            P("row", "feat"),
            P("row", "feat"),
            P("row", "rep"),
            P("row"),
            P("row", "rep", None, None),
            P("feat", None),
            P("feat", None),
        ),
        out_specs=(P(("row", "rep"), "feat"), P("feat", None), P("feat", None)),
        check_vma=False,
    )
```

```python
import jax
import jax.numpy as jnp
from jax import lax
from jax.experimental import pallas as pl
from jax.experimental.pallas import tpu as pltpu
from jax.sharding import PartitionSpec as P

BF = jnp.bfloat16
F32 = jnp.float32
VMEM_LIMIT = 48 * 2**20


def shifted(array, axis, by):
    size = lax.axis_size(axis)
    return lax.ppermute(array, axis, [(i, (i + by) % size) for i in range(size)])


def sparse_kernel(
    pos_ref, w_hbm, g_ref, sides_ref, own_ref, acc_ref, w_ref, wsem
):
    blocks, slots, size, _ = w_hbm.shape

    def wcopy(b):
        return pltpu.make_async_copy(w_hbm.at[b], w_ref.at[b], wsem.at[b])

    for b in range(blocks):
        wcopy(b).start()
    acc_ref[...] = jnp.zeros_like(acc_ref)

    @pl.loop(0, blocks)
    def _(b):
        wcopy(b).wait()
        part = pl.ds(pl.multiple_of(b * size, size), size)
        grad_t = g_ref[part, :].T
        for s in range(0, slots, 2):
            pair = jnp.concatenate([w_ref[b, s], w_ref[b, s + 1]], axis=1)
            terms = jnp.dot(grad_t, pair, preferred_element_type=F32)
            acc_ref[pos_ref[b * slots + s]] += terms[:, :size]
            acc_ref[pos_ref[b * slots + s + 1]] += terms[:, size:]

    width = g_ref.shape[1]
    pieces = blocks // own_ref.shape[0]
    for b in range(blocks):
        at = (b % pieces) * width
        for side, ref, to in ((0, sides_ref, at), (1, own_ref, at), (2, sides_ref, pieces * width + at)):
            ref[b // pieces, to : to + width, :] = acc_ref[side * blocks + b].astype(BF)


def sparse_pass(destinations, weights, grad, parts):
    blocks, slots, size, _ = weights.shape
    width = grad.shape[1]
    vmem = pl.BlockSpec(memory_space=pltpu.VMEM)
    hbm = pl.BlockSpec(memory_space=pltpu.HBM)
    smem = pl.BlockSpec(memory_space=pltpu.SMEM)
    pieces = blocks // parts
    return pl.pallas_call(
        sparse_kernel,
        in_specs=[smem, hbm, vmem],
        out_specs=[vmem] * 2,
        out_shape=[
            jax.ShapeDtypeStruct((parts, 2 * pieces * width, size), BF),
            jax.ShapeDtypeStruct((parts, pieces * width, size), BF),
        ],
        scratch_shapes=[
            pltpu.VMEM((3 * blocks + 1, width, size), F32),
            pltpu.VMEM(weights.shape, BF),
            pltpu.SemaphoreType.DMA((blocks,)),
        ],
        compiler_params=pltpu.CompilerParams(vmem_limit_bytes=VMEM_LIMIT),
        cost_estimate=pl.CostEstimate(
            flops=2 * blocks * slots * size * size * width,
            bytes_accessed=13 * 2**20,
            transcendentals=0,
        ),
    )(destinations, weights, grad)


def product_kernel(feat_ref, own_hbm, sides_hbm, *refs):
    f_hbm, (out_ref, own_ref, sides_ref, h_ref, f_ref, sem) = refs[:6], refs[6:]
    ends = [(own_hbm, own_ref), (sides_hbm, sides_ref)]
    ends += [(f_hbm[i], f_ref.at[i]) for i in range(6)]
    copies = [pltpu.make_async_copy(a, b, sem.at[i]) for i, (a, b) in enumerate(ends)]
    for copy in copies:
        copy.start()
    parts, edge, size = own_ref.shape
    width = f_ref.shape[2]
    pieces = edge // width
    copies[0].wait()
    copies[1].wait()
    for side, ref, base in ((0, sides_ref, 0), (1, own_ref, 0), (2, sides_ref, edge)):
        for b in range(parts * pieces):
            at = base + (b % pieces) * width
            h_ref[side, :, b * size : (b + 1) * size] = ref[b // pieces, at : at + width, :]
    for copy in copies[2:]:
        copy.wait()
    products = []
    for which in range(2):
        total = jnp.zeros((width, width), F32)
        for side in range(3):
            total += jnp.dot(
                h_ref[side], f_ref[side * 2 + which], preferred_element_type=F32
            )
        products.append(total)
    first = feat_ref[0] == 0
    targets = out_ref.shape[0]
    rows = width // targets
    chunks = width // size
    for f in range(2):
        value = jnp.where(first, products[f], products[1 - f])
        hi = value.astype(BF)
        lo = (value - hi.astype(F32)).astype(BF)
        for level, piece in enumerate((hi, lo)):
            for c in range(chunks):
                at = ((level * 2 + f) * chunks + c) * rows
                for t in range(targets):
                    out_ref[t, at : at + rows, :] = piece[
                        t * rows : (t + 1) * rows, c * size : (c + 1) * size
                    ]


def product(feat_index, own, sides, features, targets):
    size = own.shape[2]
    rows, width = features[0].shape
    vmem = pl.BlockSpec(memory_space=pltpu.VMEM)
    smem = pl.BlockSpec(memory_space=pltpu.SMEM)
    hbm = pl.BlockSpec(memory_space=pltpu.HBM)
    depth = 4 * (width // size) * (width // targets)
    return pl.pallas_call(
        product_kernel,
        in_specs=[smem] + [hbm] * (2 + len(features)),
        out_specs=vmem,
        out_shape=jax.ShapeDtypeStruct((targets, depth, size), BF),
        scratch_shapes=[
            pltpu.VMEM(own.shape, BF),
            pltpu.VMEM(sides.shape, BF),
            pltpu.VMEM((3, width, rows), BF),
            pltpu.VMEM((len(features), rows, width), BF),
            pltpu.SemaphoreType.DMA((2 + len(features),)),
        ],
        compiler_params=pltpu.CompilerParams(vmem_limit_bytes=VMEM_LIMIT),
        cost_estimate=pl.CostEstimate(
            flops=12 * rows * width * width, bytes_accessed=10 * 2**20, transcendentals=0
        ),
    )(feat_index, own, sides, *features)


def finish_kernel(own_ref, oth_ref, wown_ref, woth_ref, self_ref, out_ref):
    per, width, size = own_ref.shape
    for b in range(per):
        total = self_ref[b * size : (b + 1) * size, :]
        for h_ref, w_ref in ((own_ref, wown_ref), (oth_ref, woth_ref)):
            h = h_ref[b].T
            hi = h.astype(BF)
            lo = (h - hi.astype(F32)).astype(BF)
            for piece in (hi, lo):
                total += lax.dot_general(
                    piece, w_ref[...], (((1,), (1,)), ((), ())), preferred_element_type=F32
                )
        out_ref[b * size : (b + 1) * size, :] = total


def finish(h_own, h_other, w_own, w_other, self_term):
    vmem = pl.BlockSpec(memory_space=pltpu.VMEM)
    return pl.pallas_call(
        finish_kernel,
        in_specs=[vmem] * 5,
        out_specs=vmem,
        out_shape=jax.ShapeDtypeStruct(self_term.shape, F32),
        compiler_params=pltpu.CompilerParams(vmem_limit_bytes=VMEM_LIMIT),
    )(h_own, h_other, w_own, w_other, self_term)


def exchanged(value, step):
    count = lax.axis_size("row")
    return value + lax.ppermute(value, "row", [(i, i ^ step) for i in range(count)])


def whole(pieces, scaling):
    count, columns, rows, lanes = pieces.shape
    scaled = pieces.astype(F32) * scaling
    return scaled.transpose(1, 3, 0, 2).reshape(columns * lanes, count * rows)


def collect(piece):
    rows, feats = lax.axis_size("row"), lax.axis_size("feat")
    sent = jnp.broadcast_to(piece[:, None], (feats, rows) + piece.shape[1:])
    sent = sent.reshape((feats * rows,) + piece.shape[1:])
    return lax.all_to_all(sent, ("feat", "row"), 0, 0)


def local(
    features,
    grad_out,
    relu_mask,
    block_columns,
    block_count,
    block_weights,
    self_weight,
    neighbor_weight,
):
    row_devices = lax.axis_size("row")
    rep_devices = lax.axis_size("rep")
    row_index = lax.axis_index("row")
    rep_index = lax.axis_index("rep")
    feat_index = lax.axis_index("feat")
    first = feat_index == 0
    local_blocks, slot_width = block_columns.shape
    block_size = block_weights.shape[2]
    row_count, half_width = features.shape
    share_rows = row_count // rep_devices
    share_start = rep_index * share_rows
    scaling = float(row_count * row_devices) ** (-0.5)

    slot_number = rep_index * slot_width + jnp.arange(slot_width, dtype=jnp.int32)
    live_slots = slot_number[None, :] < block_count[:, None]
    relative = (block_columns // local_blocks - row_index) % row_devices
    side = jnp.where(relative == row_devices - 1, 0, jnp.where(relative == 0, 1, 2))
    destinations = jnp.where(
        live_slots, side * local_blocks + block_columns % local_blocks, 3 * local_blocks
    ).reshape(-1)

    before, after = shifted(features, "row", 1), shifted(features, "row", -1)
    features_other = shifted(features, "feat", 1)
    masked_grad = grad_out * relu_mask.astype(BF)

    lanes = block_size
    chunks = half_width // lanes
    share = half_width // rep_devices

    def self_part(values):
        whole = jnp.einsum("ro,rd->od", masked_grad, values, preferred_element_type=F32)
        mine = lax.dynamic_slice_in_dim(whole, rep_index * share, share, 0)
        return mine.reshape(share, chunks, lanes).transpose(1, 0, 2)

    self_own = self_part(features)
    self_oth = self_part(features_other)
    self_piece = jnp.stack(
        [jnp.where(first, self_own, self_oth), jnp.where(first, self_oth, self_own)]
    )
    sides, own = sparse_pass(destinations, block_weights, masked_grad, rep_devices)
    sides_got = lax.all_to_all(sides, "rep", 0, 0)
    before, after, own, self_piece = lax.optimization_barrier((before, after, own, self_piece))
    self_sum, step = self_piece, 1
    while 4 * step < row_devices:
        self_sum = exchanged(self_sum, step)
        step *= 2
    self_sum, own = lax.optimization_barrier((self_sum, own))
    if 2 * step < row_devices:
        self_sum = exchanged(self_sum, step)
        step *= 2
    extended = []
    for rows, other in ((before, None), (features, features_other), (after, None)):
        extended += [rows, shifted(rows, "feat", 1) if other is None else other]

    grad_rows = lax.dynamic_slice_in_dim(masked_grad, share_start, share_rows, 0)
    grad_rows_other = shifted(grad_rows, "feat", 1)

    def halves(weight):
        left, right = weight[:, :half_width], weight[:, half_width:]
        return jnp.where(first, left, right), jnp.where(first, right, left)

    self_w_own, self_w_oth = halves(self_weight)
    neighbor_w_own, neighbor_w_oth = halves(neighbor_weight)
    self_term = jnp.einsum(
        "ro,do->rd", grad_rows, self_w_own, preferred_element_type=F32
    ) + jnp.einsum("ro,do->rd", grad_rows_other, self_w_oth, preferred_element_type=F32)

    products = product(
        feat_index.reshape(1).astype(jnp.int32), own, sides, extended, row_devices
    )
    products, sides_got, self_sum = lax.optimization_barrier((products, sides_got, self_sum))
    products_got = lax.all_to_all(products, "row", 0, 0)
    if step < row_devices:
        self_sum = exchanged(self_sum, step)

    edge = (local_blocks // rep_devices) * half_width
    sides_sum = sides_got.astype(F32).sum(0).astype(BF)
    from_upper = shifted(sides_sum[:edge], "row", -1)
    from_lower = shifted(sides_sum[edge:], "row", 1)

    product_sum = products_got.astype(F32).sum(0).reshape(2, -1, lanes).sum(0)
    product_hi = lax.reduce_precision(product_sum, 8, 7)
    product_lo = (product_sum - product_hi).astype(BF)
    self_rows = self_sum.astype(BF).reshape(-1, lanes)
    to_all = jnp.concatenate([product_hi.astype(BF), product_lo, self_rows])
    to_all = jnp.broadcast_to(to_all[None], (rep_devices,) + to_all.shape)
    got = lax.all_to_all(jnp.concatenate([own, to_all], axis=1), "rep", 0, 0)
    middle = edge + product_sum.shape[0]
    end = middle + product_sum.shape[0]
    neighbor_piece = (got[:, edge:middle].astype(F32) + got[:, middle:end].astype(F32)).sum(0)
    neighbor_piece = neighbor_piece.reshape(2, chunks, -1, lanes)
    neighbor_grad = whole(collect(neighbor_piece.astype(BF)), scaling)

    summed = got[:, :edge].astype(F32).sum(0)
    h_own = summed + from_upper.astype(F32) + from_lower.astype(F32)
    h_own = h_own.reshape(-1, half_width, lanes)
    h_other = shifted(h_own, "feat", 1)
    features_grad = finish(h_own, h_other, neighbor_w_own, neighbor_w_oth, self_term)

    self_pieces = got[:, end:].reshape((rep_devices,) + self_sum.shape)
    keep = jnp.where(first, self_pieces[:, 0], self_pieces[:, 1])
    send = jnp.where(first, self_pieces[:, 1], self_pieces[:, 0])
    came = shifted(send, "feat", 1)
    self_grad = whole(
        jnp.concatenate([jnp.where(first, keep, came), jnp.where(first, came, keep)]), scaling
    )
    return (features_grad, self_grad, neighbor_grad)


def solution(mesh):
    return jax.shard_map(
        local,
        mesh=mesh,
        in_specs=(
            P("row", "feat"),
            P("row", "feat"),
            P("row", "feat"),
            P("row", "rep"),
            P("row"),
            P("row", "rep", None, None),
            P("feat", None),
            P("feat", None),
        ),
        out_specs=(P(("row", "rep"), "feat"), P("feat", None), P("feat", None)),
        check_vma=False,
    )
```
